32 devices in a mesh: parts: 2 (over y), fsdp: 16 (over z, x, core).
Axes of the slice: x: 2, y: 2, z: 4, core: 2. Of those that a mesh axis runs over, the one named last changes fastest.
Arguments:
- token_inputs_stacked: bfloat16 [8192, 8192], P(('parts', 'fsdp')), parts along dimension 0, may hold values from -6 to 6
- cotangent: bfloat16 [8192, 8192], P(('parts', 'fsdp')), parts along dimension 0, may hold values from -6 to 6
- ascending_adapter_matrix: bfloat16 [8192, 128], P('fsdp'), may hold values from -0.0625 to 0.0625
- narrow_sketch_matrix: bfloat16 [128, 16], replicated, may hold values from -0.5 to 0.5
- input_side_projection: bfloat16 [8192, 512], P('fsdp'), may hold values from -0.0625 to 0.0625
- lengths: int32 [64], P(('parts', 'fsdp')), parts along dimension 0, may hold values from 1 to 128
Outputs:
- features: float32 [64, 8192], P(('parts', 'fsdp')), parts along dimension 0
- gram: float32 [16384, 8192], P(('parts', 'fsdp')), parts along dimension 0
The draws below stay inside these ranges and needn't reach their ends.
There are 2 independent parts, one for each index of `parts`. The reference program is written for one: setup_inputs(seed, part) draws one part's arguments, and reference() takes and returns one part's arrays. A program takes and returns all parts, laid end to end along the dimension named above; an argument that names none is the same for every part. Nothing has to cross between parts.
All inputs are finite; a program needn't handle non-finite values.
Results may differ from the reference program's by a relative error of at most 0.007.
Values may be sent and summed in bfloat16 or wider, within the bound.
A program may use at most 128 MiB of HBM per device.

```python
import math
import jax
import jax.numpy as jnp
from jax import lax

EMBED_DIM = 8192
ADAPTER_DIM = 128
SKETCH_COLS_R = 16
KD = 512
SEQ = 128
EX = 32
TOKENS = 4096


def touch_ends(values, rng, low, top_value):
    longest = values.shape.index(max(values.shape))
    spots = []
    for shift in (0, 1):
        where = [jax.random.randint(jax.random.fold_in(rng, axis), (), 0, length) for axis, length in enumerate(values.shape)]
        where[longest] = (where[longest] + shift) % values.shape[longest]
        spots.append(tuple(where))
    return values.at[spots[0]].set(low).at[spots[1]].set(top_value)


def shard_levels(rng, dims, pieces, least, largest):
    loudness = 1.0
    for dim, blocks in pieces:
        heights = jax.random.uniform(jax.random.fold_in(jax.random.fold_in(rng, 6), dim), (blocks,), jnp.float32, least / len(pieces), largest / len(pieces))
        loudness = loudness * jnp.repeat(jnp.exp(heights), dims[dim] // blocks).reshape((-1,) + (1,) * (len(dims) - 1 - dim))
    return loudness


def noise(rng, extent, width, most, split=(), held_as=jnp.bfloat16):
    result = width * jax.random.normal(rng, extent, jnp.float32)
    if split:
        result = result * shard_levels(rng, extent, split, -0.22, 0.18)
    return jnp.clip(result, -most, most).astype(held_as)


def setup_inputs(seed: int = 0, part: int = 0) -> dict:
    seeds = jax.random.split(jax.random.key(seed), 7)
    part_splits = jax.random.split(jax.random.fold_in(seeds[6], part), 7)
    token_inputs_stacked = noise(part_splits[0], (TOKENS, EMBED_DIM), 1.0, 6.0, ((0, 16),))
    cotangent = noise(part_splits[1], (TOKENS, EMBED_DIM), 1.0, 6.0, ((0, 16),))
    ascending_adapter_matrix = noise(seeds[2], (EMBED_DIM, ADAPTER_DIM), EMBED_DIM ** -0.5, 0.0625, ((0, 16),))
    narrow_sketch_matrix = noise(seeds[3], (ADAPTER_DIM, SKETCH_COLS_R), ADAPTER_DIM ** -0.5, 0.5)
    input_side_projection = noise(seeds[4], (EMBED_DIM, KD), EMBED_DIM ** -0.5, 0.0625, ((0, 16),))
    lengths = touch_ends(jax.random.randint(part_splits[5], (EX,), 1, SEQ + 1), jax.random.fold_in(part_splits[5], 1), 1, SEQ).astype(jnp.int32)
    return {"token_inputs_stacked": token_inputs_stacked, "cotangent": cotangent, "ascending_adapter_matrix": ascending_adapter_matrix, "narrow_sketch_matrix": narrow_sketch_matrix, "input_side_projection": input_side_projection, "lengths": lengths}


def outer_features(sketch_block, input_block):
    ex_n = sketch_block.shape[0]
    seq_n = sketch_block.shape[1]
    wide = input_block.reshape(ex_n, seq_n, -1)
    joined = jnp.einsum('esr,esk->erk', sketch_block.astype(jnp.float32), wide, precision=lax.Precision.HIGHEST)
    return joined.reshape(ex_n, -1) * (1.0 / math.sqrt(seq_n))

def reference(token_inputs_stacked, cotangent, ascending_adapter_matrix, narrow_sketch_matrix, input_side_projection, lengths):
    hidden_state = jnp.dot(cotangent, ascending_adapter_matrix, preferred_element_type=jnp.float32).astype(jnp.bfloat16)
    live_mask = (jnp.arange(SEQ, dtype=jnp.int32)[None, :] < lengths[:, None]).astype(jnp.float32)
    sketch = jnp.dot(hidden_state, narrow_sketch_matrix, preferred_element_type=jnp.float32).reshape(EX, SEQ, SKETCH_COLS_R)
    sketch = (sketch * live_mask[:, :, None]).astype(jnp.bfloat16)
    group_size = math.gcd(EX, 32)
    block_rows = token_inputs_stacked.reshape(EX // group_size, group_size * SEQ, EMBED_DIM)
    block_sketch = sketch.reshape(EX // group_size, group_size, SEQ, SKETCH_COLS_R)

    def one_group(operands):
        sketched_entries = jnp.dot(operands[0], input_side_projection, preferred_element_type=jnp.float32)
        return outer_features(operands[1], sketched_entries)
    features = lax.map(one_group, (block_rows, block_sketch)).reshape(EX, SKETCH_COLS_R * KD)
    rounded = features.astype(jnp.bfloat16)
    gram = lax.dot_general(rounded, rounded, (((0,), (0,)), ((), ())), preferred_element_type=jnp.float32)
    return (features, gram * (1.0 / EX))
```

```python
import math

import jax
import jax.numpy as jnp
from jax import lax
from jax.sharding import PartitionSpec as P


def halves(value, axis):
    high = value.astype(jnp.bfloat16)
    low = (value - high.astype(jnp.float32)).astype(jnp.bfloat16)
    return jnp.concatenate([high, low], axis=axis)


def on_device(inputs, cotangent, up, narrow, projection, lengths):
    position = lax.axis_index("fsdp")
    devices_n = lax.axis_size("fsdp")
    ex_dev = lengths.shape[0]
    seq_len = inputs.shape[0] // ex_dev
    rank = narrow.shape[1]
    f32 = jnp.float32
    folded = lax.dot_general(narrow, up, (((0,), (1,)), ((), ())), preferred_element_type=f32)
    folded = lax.all_gather(halves(folded, 0), "fsdp", axis=1, tiled=True)
    sketch = lax.dot_general(cotangent, folded, (((1,), (1,)), ((), ())), preferred_element_type=f32)
    sketch = sketch[:, :rank] + sketch[:, rank:]
    live = jnp.arange(seq_len, dtype=jnp.int32)[None, :] < lengths[:, None]
    sketch = jnp.where(live[:, :, None], sketch.reshape(ex_dev, seq_len, rank), 0.0)
    wide = inputs.reshape(ex_dev, seq_len, -1)
    mixed = jnp.einsum("esr,esd->erd", halves(sketch, 2), wide, preferred_element_type=f32)
    mixed = (mixed[:, :rank] + mixed[:, rank:]).astype(jnp.bfloat16)
    mixed = mixed.reshape(ex_dev * rank, -1)
    mixed = lax.all_to_all(mixed, "fsdp", split_axis=1, concat_axis=0, tiled=True)
    part = jnp.dot(mixed, projection, preferred_element_type=f32)
    features = lax.psum_scatter(part, "fsdp", scatter_dimension=0, tiled=True)
    features = features.reshape(ex_dev, -1) * (1.0 / math.sqrt(seq_len))
    rounded = features.astype(jnp.bfloat16)
    own_rows = rounded.shape[1] // devices_n
    all_rows = lax.all_gather(rounded, "fsdp", axis=0, tiled=True)
    own_cols = lax.dynamic_slice_in_dim(all_rows, position * own_rows, own_rows, 1)
    gram = lax.dot_general(
        own_cols, all_rows, (((0,), (0,)), ((), ())), preferred_element_type=f32
    )
    return features, gram * (1.0 / (ex_dev * devices_n))


def solution(mesh):
    rows = P(("parts", "fsdp"), None)
    in_specs = (rows, rows, P("fsdp", None), P(), P("fsdp", None), P(("parts", "fsdp")))
    return jax.shard_map(
        on_device, mesh=mesh, in_specs=in_specs, out_specs=(rows, rows), check_vma=False
    )
```

```python
import functools
import math

import jax
import jax.numpy as jnp
from jax import lax
from jax.experimental import pallas as pl
from jax.experimental.pallas import tpu as pltpu
from jax.sharding import PartitionSpec as P

BF = jnp.bfloat16
F32 = jnp.float32
NT = (((1,), (1,)), ((), ()))


def halves(value):
    high = value.astype(BF)
    low = (value - high.astype(F32)).astype(BF)
    return jnp.concatenate([high, low], axis=0)


def features_kernel(
    outer,
    len_ref, up_ref, narrow_ref, proj_ref, cot_hbm, x_hbm,
    feat_ref, all_ref,
    cot, x, folded, pin, ysend, yrecv, psend, precv,
    local_sem, bz_s, bz_r, bb_s, bb_r, bc_s, bc_r,
    fz_s, fz_r, fb_s, fb_r, fc_s, fc_r, pin_s, pin_r, y_s, y_r, p_s, p_r,
):
    me = lax.axis_index("fsdp")
    o, within = me // 4, me % 4
    b, c = within // 2, within % 2
    plane = within
    mate_b = o * 4 + (1 - b) * 2 + c
    mate_c = o * 4 + b * 2 + (1 - c)
    rank = narrow_ref.shape[1]
    ex = len_ref.shape[0]
    seq = x.shape[0] // ex
    wide = ysend.shape[2]

    def along(step):
        return lax.rem(o + step, outer) * 4 + plane

    loads = [
        pltpu.make_async_copy(cot_hbm, cot, local_sem.at[0]),
        pltpu.make_async_copy(x_hbm, x, local_sem.at[1]),
        pltpu.make_async_copy(proj_ref, pin.at[plane], local_sem.at[2]),
    ]
    for load in loads:
        load.start()

    barrier = pltpu.get_barrier_semaphore()
    for other in [along(k) for k in range(1, outer)] + [mate_b, mate_c]:
        pl.semaphore_signal(
            barrier, inc=1, device_id={"fsdp": other}, device_id_type=pl.DeviceIdType.MESH
        )

    part = lax.dot_general(
        narrow_ref[...], up_ref[...], (((0,), (1,)), ((), ())), preferred_element_type=F32
    )
    folded[me] = halves(part)
    pl.semaphore_wait(barrier, outer + 1)

    sent = []

    def send(src, dst, s_sem, r_sem, other):
        copy = pltpu.make_async_remote_copy(
            src_ref=src, dst_ref=dst, send_sem=s_sem, recv_sem=r_sem,
            device_id={"fsdp": other}, device_id_type=pl.DeviceIdType.MESH,
        )
        copy.start()
        sent.append(copy)

    def arrived(dst, sem):
        pltpu.make_async_copy(dst, dst, sem).wait()

    def gather(buf, z_s, z_r, b_s, b_r, c_s, c_r):
        for k in range(1, outer):
            send(buf.at[me], buf.at[me], z_s.at[k], z_r.at[k], along(k))
        send(buf.at[me], buf.at[me], b_s.at[0], b_r.at[0], mate_b)
        send(buf.at[me], buf.at[me], c_s.at[0], c_r.at[0], mate_c)
        for k in range(1, outer):
            slot = along(outer - k)
            arrived(buf.at[slot], z_r.at[k])
            send(buf.at[slot], buf.at[slot], b_s.at[k], b_r.at[k], mate_b)
            send(buf.at[slot], buf.at[slot], c_s.at[k], c_r.at[k], mate_c)
        for k in range(outer):
            slot = lax.rem(o + outer - k, outer) * 4 + (1 - b) * 2 + c
            arrived(buf.at[slot], b_r.at[k])
            send(buf.at[slot], buf.at[slot], c_s.at[outer + k], c_r.at[outer + k], mate_c)
        for half in range(2):
            for k in range(outer):
                arrived(buf.at[me], c_r.at[half * outer + k])

    def pin_start():
        send(proj_ref, pin.at[plane], pin_s.at[0], pin_r.at[0], mate_b)
        send(proj_ref, pin.at[plane], pin_s.at[1], pin_r.at[1], mate_c)

    pin_start()
    gather(folded, bz_s, bz_r, bb_s, bb_r, bc_s, bc_r)

    loads[0].wait()
    sketch = jnp.zeros((2 * rank, x.shape[0]), F32)
    for i in range(outer):
        block = jnp.concatenate([folded[i * 4 + j] for j in range(4)], axis=1)
        sketch += lax.dot_general(
            block, cot[:, i * wide:(i + 1) * wide], NT, preferred_element_type=F32
        )
    sketch = sketch[:rank] + sketch[rank:]
    tok = lax.broadcasted_iota(jnp.int32, (rank, seq), 1)
    mixers = [
        halves(jnp.where(tok < len_ref[e], sketch[:, e * seq:(e + 1) * seq], 0.0))
        for e in range(ex)
    ]

    loads[1].wait()
    for k in list(range(1, outer)) + [0]:
        cols = pl.ds(pl.multiple_of(lax.rem(o + k, outer) * wide, wide), wide)
        for e in range(ex):
            mixed = jnp.dot(
                mixers[e], x[e * seq:(e + 1) * seq, cols], preferred_element_type=F32
            )
            ysend[k, e * rank:(e + 1) * rank] = (mixed[:rank] + mixed[rank:]).astype(BF)
        if k:
            send(ysend.at[k], yrecv.at[k], y_s.at[k], y_r.at[k], along(k))

    loads[2].wait()
    across = (1 - b) * 2 + c
    arrived(pin.at[across], pin_r.at[0])
    send(pin.at[across], pin.at[across], pin_s.at[2], pin_r.at[2], mate_c)
    arrived(pin.at[b * 2 + 1 - c], pin_r.at[1])
    arrived(pin.at[(1 - b) * 2 + 1 - c], pin_r.at[2])

    def project(value):
        depth = wide // 4
        total = jnp.zeros((ex * rank, pin.shape[2]), F32)
        for j in range(4):
            total += jnp.dot(
                value[:, j * depth:(j + 1) * depth], pin[j], preferred_element_type=F32
            )
        return total

    total = project(ysend[0])
    for k in range(1, outer):
        arrived(yrecv.at[k], y_r.at[k])
        psend[k] = project(yrecv[k])
        send(psend.at[k], precv.at[k], p_s.at[k], p_r.at[k], along(outer - k))
    for k in range(1, outer):
        arrived(precv.at[k], p_r.at[k])
        total += precv[k]
    total = total * (1.0 / math.sqrt(seq))
    feat_ref[...] = total
    all_ref[me] = total.astype(BF)
    gather(all_ref, fz_s, fz_r, fb_s, fb_r, fc_s, fc_r)
    for copy in sent:
        copy.wait_send()


def gram_kernel(ex, all_ref, feat32_ref, gram_ref, feat_ref, rows, few, own):
    me = lax.axis_index("fsdp")
    step = pl.program_id(0)
    own_rows, kd = gram_ref.shape
    chunks, height, lanes = rows.shape
    rank = height // (all_ref.shape[0] * ex)
    total = height // rank

    def row_of(ref, r, count):
        return jnp.concatenate(
            [ref[i, pl.ds(r, count, stride=rank), :] for i in range(chunks)], axis=1
        )

    @pl.when(step == 0)
    def _():
        for i in range(chunks):
            cols = slice(i * lanes, (i + 1) * lanes)
            rows[i] = all_ref[:, :, cols].reshape(height, lanes).astype(F32)
            few[i] = feat32_ref[:, cols]
        own[...] = row_of(rows, me * own_rows // kd, total).T
        for r in range(rank):
            feat_ref[:, r * kd:(r + 1) * kd] = row_of(few, r, ex)

    left = own[pl.ds(pl.multiple_of(lax.rem(me * own_rows, kd), own_rows), own_rows), :]
    gram_ref[...] = jnp.dot(
        left.astype(BF), row_of(rows, step, total).astype(BF), preferred_element_type=F32
    ) * (1.0 / total)


def on_device(inputs, cotangent, up, narrow, projection, lengths):
    devices = lax.axis_size("fsdp")
    outer = devices // 4
    ex = lengths.shape[0]
    tokens, width = inputs.shape
    rank = narrow.shape[1]
    depth, kd = projection.shape
    rows = ex * rank
    vmem = pl.BlockSpec(memory_space=pltpu.VMEM)
    anywhere = pl.BlockSpec(memory_space=pl.ANY)
    sems = [3]
    sems += [outer, outer, outer, outer, 2 * outer, 2 * outer] * 2
    sems += [3, 3, outer, outer, outer, outer]
    feat32, everyone = pl.pallas_call(
        functools.partial(features_kernel, outer),
        out_shape=(
            jax.ShapeDtypeStruct((rows, kd), F32),
            jax.ShapeDtypeStruct((devices, rows, kd), BF),
        ),
        in_specs=[
            pl.BlockSpec(memory_space=pltpu.SMEM), vmem, vmem, anywhere, anywhere, anywhere
        ],
        out_specs=(vmem, vmem),
        scratch_shapes=[
            pltpu.VMEM((tokens, width), BF),
            pltpu.VMEM((tokens, width), BF),
            pltpu.VMEM((devices, 2 * rank, depth), BF),
            pltpu.VMEM((4, depth, kd), BF),
            pltpu.VMEM((outer, rows, 4 * depth), BF),
            pltpu.VMEM((outer, rows, 4 * depth), BF),
            pltpu.VMEM((outer, rows, kd), F32),
            pltpu.VMEM((outer, rows, kd), F32),
        ] + [pltpu.SemaphoreType.DMA((n,)) for n in sems],
        compiler_params=pltpu.CompilerParams(
            collective_id=0, has_side_effects=True, vmem_limit_bytes=48 * 1024 * 1024
        ),
        name="features",
    )(lengths, up, narrow, projection, cotangent, inputs)
    own_rows = rank * kd // devices
    total = ex * devices
    gram, features = pl.pallas_call(
        functools.partial(gram_kernel, ex),
        grid=(rank,),
        out_shape=(
            jax.ShapeDtypeStruct((own_rows, rank * kd), F32),
            jax.ShapeDtypeStruct((ex, rank * kd), F32),
        ),
        in_specs=[
            pl.BlockSpec((devices, rows, kd), lambda i: (0, 0, 0)),
            pl.BlockSpec((rows, kd), lambda i: (0, 0)),
        ],
        out_specs=(
            pl.BlockSpec((own_rows, kd), lambda i: (0, i)),
            pl.BlockSpec((ex, rank * kd), lambda i: (0, 0)),
        ),
        scratch_shapes=[
            pltpu.VMEM((kd // 128, total * rank, 128), F32),
            pltpu.VMEM((kd // 128, rows, 128), F32),
            pltpu.VMEM((kd, total), F32),
        ],
        compiler_params=pltpu.CompilerParams(vmem_limit_bytes=48 * 1024 * 1024),
        name="gram",
    )(everyone, feat32)
    return features, gram


def solution(mesh):
    rows = P(("parts", "fsdp"), None)
    in_specs = (rows, rows, P("fsdp", None), P(), P("fsdp", None), P(("parts", "fsdp")))
    return jax.shard_map(
        on_device, mesh=mesh, in_specs=in_specs, out_specs=(rows, rows), check_vma=False
    )
```

```python
import functools
import math

import jax
import jax.numpy as jnp
from jax import lax
from jax.experimental import pallas as pl
from jax.experimental.pallas import tpu as pltpu
from jax.sharding import PartitionSpec as P

BF = jnp.bfloat16
F32 = jnp.float32
NT = (((1,), (1,)), ((), ()))


def halves(value):
    high = value.astype(BF)
    low = (value - high.astype(F32)).astype(BF)
    return jnp.concatenate([high, low], axis=0)


def features_kernel(
    outer,
    len_hbm, up_hbm, narrow_hbm, proj_ref, cot_hbm, x_hbm,
    feat_ref, all_ref,
    len_ref, up_ref, narrow_ref, cot, x, folded, pin, ysend, yrecv, psend, precv,
    local_sem, bz_s, bz_r, bb_s, bb_r, bc_s, bc_r,
    fz_s, fz_r, fb_s, fb_r, fc_s, fc_r, pin_s, pin_r, y_s, y_r, p_s, p_r,
):
    me = lax.axis_index("fsdp")
    o, within = me // 4, me % 4
    b, c = within // 2, within % 2
    plane = within
    mate_b = o * 4 + (1 - b) * 2 + c
    mate_c = o * 4 + b * 2 + (1 - c)
    rank = narrow_ref.shape[0]
    ex = len_ref.shape[0]
    seq = x.shape[0] // ex
    wide = ysend.shape[2]

    def along(step):
        return lax.rem(o + step, outer) * 4 + plane

    early = [
        pltpu.make_async_copy(up_hbm, up_ref, local_sem.at[3]),
        pltpu.make_async_copy(narrow_hbm, narrow_ref, local_sem.at[4]),
        pltpu.make_async_copy(len_hbm, len_ref, local_sem.at[5]),
    ]
    loads = [
        pltpu.make_async_copy(cot_hbm, cot, local_sem.at[0]),
        pltpu.make_async_copy(x_hbm, x, local_sem.at[1]),
        pltpu.make_async_copy(proj_ref, pin.at[plane], local_sem.at[2]),
    ]
    for load in early + loads:
        load.start()

    barrier = pltpu.get_barrier_semaphore()
    for other in [along(k) for k in range(1, outer)] + [mate_b, mate_c]:
        pl.semaphore_signal(
            barrier, inc=1, device_id={"fsdp": other}, device_id_type=pl.DeviceIdType.MESH
        )

    for load in early:
        load.wait()
    part = lax.dot_general(narrow_ref[...], up_ref[...], NT, preferred_element_type=F32)
    folded[me] = halves(part)
    pl.semaphore_wait(barrier, outer + 1)

    sent = []

    def send(src, dst, s_sem, r_sem, other):
        copy = pltpu.make_async_remote_copy(
            src_ref=src, dst_ref=dst, send_sem=s_sem, recv_sem=r_sem,
            device_id={"fsdp": other}, device_id_type=pl.DeviceIdType.MESH,
        )
        copy.start()
        sent.append(copy)

    def arrived(dst, sem):
        pltpu.make_async_copy(dst, dst, sem).wait()

    def gather(buf, z_s, z_r, b_s, b_r, c_s, c_r):
        for k in range(1, outer):
            send(buf.at[me], buf.at[me], z_s.at[k], z_r.at[k], along(k))
        send(buf.at[me], buf.at[me], b_s.at[0], b_r.at[0], mate_b)
        send(buf.at[me], buf.at[me], c_s.at[0], c_r.at[0], mate_c)
        for k in range(1, outer):
            slot = along(outer - k)
            arrived(buf.at[slot], z_r.at[k])
            send(buf.at[slot], buf.at[slot], b_s.at[k], b_r.at[k], mate_b)
            send(buf.at[slot], buf.at[slot], c_s.at[k], c_r.at[k], mate_c)
        for k in range(outer):
            slot = lax.rem(o + outer - k, outer) * 4 + (1 - b) * 2 + c
            arrived(buf.at[slot], b_r.at[k])
            send(buf.at[slot], buf.at[slot], c_s.at[outer + k], c_r.at[outer + k], mate_c)
        for half in range(2):
            for k in range(outer):
                arrived(buf.at[me], c_r.at[half * outer + k])

    depth = wide // 4
    pieces = 4
    high = depth // pieces

    def piece(slot, i):
        return pin.at[slot, pl.ds(i * high, high)]

    def pin_start(i):
        source = proj_ref.at[pl.ds(i * high, high)]
        send(source, piece(plane, i), pin_s.at[0, i], pin_r.at[0, i], mate_b)

    pin_start(0)
    gather(folded, bz_s, bz_r, bb_s, bb_r, bc_s, bc_r)
    for i in range(1, pieces):
        pin_start(i)
    send(proj_ref, pin.at[plane], pin_s.at[1, 0], pin_r.at[1, 0], mate_c)

    loads[0].wait()
    sketch = jnp.zeros((2 * rank, x.shape[0]), F32)
    for i in range(outer):
        block = jnp.concatenate([folded[i * 4 + j] for j in range(4)], axis=1)
        sketch += lax.dot_general(
            block, cot[:, i * wide:(i + 1) * wide], NT, preferred_element_type=F32
        )
    sketch = sketch[:rank] + sketch[rank:]
    tok = lax.broadcasted_iota(jnp.int32, (rank, seq), 1)
    mixers = [
        halves(jnp.where(tok < len_ref[e], sketch[:, e * seq:(e + 1) * seq], 0.0))
        for e in range(ex)
    ]

    loads[1].wait()
    for k in list(range(1, outer)) + [0]:
        cols = pl.ds(pl.multiple_of(lax.rem(o + k, outer) * wide, wide), wide)
        for e in range(ex):
            mixed = jnp.dot(
                mixers[e], x[e * seq:(e + 1) * seq, cols], preferred_element_type=F32
            )
            mixed = (mixed[:rank] + mixed[rank:]).astype(BF)
            if k:
                ysend[k, e * rank:(e + 1) * rank] = mixed
            else:
                yrecv[k, e * rank:(e + 1) * rank] = mixed
        if k:
            send(ysend.at[k], yrecv.at[k], y_s.at[k], y_r.at[k], along(k))

    loads[2].wait()
    across = (1 - b) * 2 + c
    for i in range(pieces):
        arrived(piece(across, i), pin_r.at[0, i])
        send(piece(across, i), piece(across, i), pin_s.at[2, i], pin_r.at[2, i], mate_c)
    arrived(pin.at[b * 2 + 1 - c], pin_r.at[1, 0])
    for i in range(pieces):
        arrived(piece((1 - b) * 2 + 1 - c, i), pin_r.at[2, i])
    for k in range(1, outer):
        arrived(yrecv.at[k], y_r.at[k])

    mixed = yrecv[...].reshape(outer * ex * rank, wide)
    parts = jnp.zeros((outer * ex * rank, pin.shape[2]), F32)
    for j in range(4):
        parts += jnp.dot(
            mixed[:, j * depth:(j + 1) * depth], pin[j], preferred_element_type=F32
        )
    for k in range(1, outer):
        psend[k] = parts[k * ex * rank:(k + 1) * ex * rank].astype(BF)
        send(psend.at[k], precv.at[k], p_s.at[k], p_r.at[k], along(outer - k))
    total = parts[:ex * rank]
    for k in range(1, outer):
        arrived(precv.at[k], p_r.at[k])
        total += precv[k].astype(F32)
    total = total * (1.0 / math.sqrt(seq))
    feat_ref[...] = total
    all_ref[me] = total.astype(BF)
    gather(all_ref, fz_s, fz_r, fb_s, fb_r, fc_s, fc_r)
    for copy in sent:
        copy.wait_send()


def gram_kernel(ex, all_ref, feat32_ref, gram_hbm, feat_ref, rows, few, own, tiles, sems):
    me = lax.axis_index("fsdp")
    _, own_rows, kd = tiles.shape
    chunks, height, lanes = rows.shape
    rank = height // (all_ref.shape[0] * ex)
    total = height // rank

    def row_of(ref, r, count):
        return jnp.concatenate(
            [ref[i, pl.ds(r, count, stride=rank), :] for i in range(chunks)], axis=1
        )

    for i in range(chunks):
        cols = slice(i * lanes, (i + 1) * lanes)
        rows[i] = all_ref[:, :, cols].reshape(height, lanes).astype(F32)
        few[i] = feat32_ref[:, cols]
    own[...] = row_of(rows, me * own_rows // kd, total).T
    left = own[pl.ds(pl.multiple_of(lax.rem(me * own_rows, kd), own_rows), own_rows), :]
    left = left.astype(BF)
    writes = []
    for r in range(rank):
        tiles[r] = jnp.dot(
            left, row_of(rows, r, total).astype(BF), preferred_element_type=F32
        ) * (1.0 / total)
        write = pltpu.make_async_copy(
            tiles.at[r], gram_hbm.at[:, r * kd:(r + 1) * kd], sems.at[r]
        )
        write.start()
        writes.append(write)
    for r in range(rank):
        feat_ref[:, r * kd:(r + 1) * kd] = row_of(few, r, ex)
    for write in writes:
        write.wait()


def on_device(inputs, cotangent, up, narrow, projection, lengths):
    devices = lax.axis_size("fsdp")
    outer = devices // 4
    ex = lengths.shape[0]
    tokens, width = inputs.shape
    rank = narrow.shape[1]
    depth, kd = projection.shape
    rows = ex * rank
    vmem = pl.BlockSpec(memory_space=pltpu.VMEM)
    hbm = pl.BlockSpec(memory_space=pltpu.HBM)
    sems = [6]
    sems += [outer, outer, outer, outer, 2 * outer, 2 * outer] * 2
    sems += [(3, 4), (3, 4), outer, outer, outer, outer]
    feat32, everyone = pl.pallas_call(
        functools.partial(features_kernel, outer),
        out_shape=(
            jax.ShapeDtypeStruct((rows, kd), F32),
            jax.ShapeDtypeStruct((devices, rows, kd), BF),
        ),
        in_specs=[hbm] * 6,
        out_specs=(vmem, vmem),
        scratch_shapes=[
            pltpu.SMEM((ex,), jnp.int32),
            pltpu.VMEM((depth, up.shape[1]), BF),
            pltpu.VMEM((rank, up.shape[1]), BF),
            pltpu.VMEM((tokens, width), BF),
            pltpu.VMEM((tokens, width), BF),
            pltpu.VMEM((devices, 2 * rank, depth), BF),
            pltpu.VMEM((4, depth, kd), BF),
            pltpu.VMEM((outer, rows, 4 * depth), BF),
            pltpu.VMEM((outer, rows, 4 * depth), BF),
            pltpu.VMEM((outer, rows, kd), BF),
            pltpu.VMEM((outer, rows, kd), BF),
        ] + [pltpu.SemaphoreType.DMA(n if isinstance(n, tuple) else (n,)) for n in sems],
        compiler_params=pltpu.CompilerParams(
            collective_id=0, has_side_effects=True, vmem_limit_bytes=63 * 1024 * 1024
        ),
        name="features",
    )(lengths, up, narrow.T, projection, cotangent, inputs)
    own_rows = rank * kd // devices
    total = ex * devices
    gram, features = pl.pallas_call(
        functools.partial(gram_kernel, ex),
        out_shape=(
            jax.ShapeDtypeStruct((own_rows, rank * kd), F32),
            jax.ShapeDtypeStruct((ex, rank * kd), F32),
        ),
        in_specs=[vmem, vmem],
        out_specs=(hbm, vmem),
        scratch_shapes=[
            pltpu.VMEM((kd // 128, total * rank, 128), F32),
            pltpu.VMEM((kd // 128, rows, 128), F32),
            pltpu.VMEM((kd, total), F32),
            pltpu.VMEM((rank, own_rows, kd), F32),
            pltpu.SemaphoreType.DMA((rank,)),
        ],
        compiler_params=pltpu.CompilerParams(vmem_limit_bytes=63 * 1024 * 1024),
        name="gram",
    )(everyone, feat32)
    return features, gram


def solution(mesh):
    rows = P(("parts", "fsdp"), None)
    in_specs = (rows, rows, P("fsdp", None), P(), P("fsdp", None), P(("parts", "fsdp")))
    return jax.shard_map(
        on_device, mesh=mesh, in_specs=in_specs, out_specs=(rows, rows), check_vma=False
    )
```

```python
import functools
import math

import jax
import jax.numpy as jnp
from jax import lax
from jax.experimental import pallas as pl
from jax.experimental.pallas import tpu as pltpu
from jax.sharding import PartitionSpec as P

BF = jnp.bfloat16
F32 = jnp.float32
NT = (((1,), (1,)), ((), ()))


def halves(value):
    high = value.astype(BF)
    low = (value - high.astype(F32)).astype(BF)
    return jnp.concatenate([high, low], axis=0)


def features_kernel(
    outer,
    len_hbm, up_hbm, narrow_hbm, proj_ref, cot_hbm, x_hbm,
    feat_ref, all_ref,
    len_ref, up_ref, narrow_ref, cot, x, folded, pin, ysend, yrecv, psend, precv,
    local_sem, bz_s, bz_r, bb_s, bb_r, bc_s, bc_r,
    fz_s, fz_r, fb_s, fb_r, fc_s, fc_r, pin_s, pin_r, y_s, y_r, p_s, p_r,
):
    me = lax.axis_index("fsdp")
    o, within = me // 4, me % 4
    b, c = within // 2, within % 2
    plane = within
    mate_b = o * 4 + (1 - b) * 2 + c
    mate_c = o * 4 + b * 2 + (1 - c)
    rank = narrow_ref.shape[0]
    ex = len_ref.shape[0]
    seq = x.shape[0] // ex
    wide = ysend.shape[2]

    def along(step):
        return lax.rem(o + step, outer) * 4 + plane

    early = [
        pltpu.make_async_copy(up_hbm, up_ref, local_sem.at[3]),
        pltpu.make_async_copy(narrow_hbm, narrow_ref, local_sem.at[4]),
        pltpu.make_async_copy(len_hbm, len_ref, local_sem.at[5]),
    ]
    loads = [
        pltpu.make_async_copy(cot_hbm, cot, local_sem.at[0]),
        pltpu.make_async_copy(x_hbm, x, local_sem.at[1]),
        pltpu.make_async_copy(proj_ref, pin.at[plane], local_sem.at[2]),
    ]
    for load in early + loads:
        load.start()

    barrier = pltpu.get_barrier_semaphore()
    for other in [along(k) for k in range(1, outer)] + [mate_b, mate_c]:
        pl.semaphore_signal(
            barrier, inc=1, device_id={"fsdp": other}, device_id_type=pl.DeviceIdType.MESH
        )

    for load in early:
        load.wait()
    part = lax.dot_general(narrow_ref[...], up_ref[...], NT, preferred_element_type=F32)
    folded[me] = halves(part)
    pl.semaphore_wait(barrier, outer + 1)

    sent = []
    order = sorted(range(1, outer), key=lambda k: abs(k - outer // 2))

    def send(src, dst, s_sem, r_sem, other):
        copy = pltpu.make_async_remote_copy(
            src_ref=src, dst_ref=dst, send_sem=s_sem, recv_sem=r_sem,
            device_id={"fsdp": other}, device_id_type=pl.DeviceIdType.MESH,
        )
        copy.start()
        sent.append(copy)

    def arrived(dst, sem):
        pltpu.make_async_copy(dst, dst, sem).wait()

    def gather(buf, z_s, z_r, b_s, b_r, c_s, c_r):
        for k in range(1, outer):
            send(buf.at[me], buf.at[me], z_s.at[k], z_r.at[k], along(k))
        send(buf.at[me], buf.at[me], b_s.at[0], b_r.at[0], mate_b)
        send(buf.at[me], buf.at[me], c_s.at[0], c_r.at[0], mate_c)
        for k in reversed(order):
            slot = along(outer - k)
            arrived(buf.at[slot], z_r.at[k])
            send(buf.at[slot], buf.at[slot], b_s.at[k], b_r.at[k], mate_b)
            send(buf.at[slot], buf.at[slot], c_s.at[k], c_r.at[k], mate_c)
        for k in range(outer):
            slot = lax.rem(o + outer - k, outer) * 4 + (1 - b) * 2 + c
            arrived(buf.at[slot], b_r.at[k])
            send(buf.at[slot], buf.at[slot], c_s.at[outer + k], c_r.at[outer + k], mate_c)
        for half in range(2):
            for k in range(outer):
                arrived(buf.at[me], c_r.at[half * outer + k])

    depth = wide // 4
    pieces = 4
    high = depth // pieces

    def piece(slot, i):
        return pin.at[slot, pl.ds(i * high, high)]

    def pin_start(i):
        source = proj_ref.at[pl.ds(i * high, high)]
        send(source, piece(plane, i), pin_s.at[0, i], pin_r.at[0, i], mate_b)

    pin_start(0)
    gather(folded, bz_s, bz_r, bb_s, bb_r, bc_s, bc_r)
    for i in range(1, pieces):
        pin_start(i)
    send(proj_ref, pin.at[plane], pin_s.at[1, 0], pin_r.at[1, 0], mate_c)

    loads[0].wait()
    sketch = jnp.zeros((2 * rank, x.shape[0]), F32)
    for i in range(outer):
        block = jnp.concatenate([folded[i * 4 + j] for j in range(4)], axis=1)
        sketch += lax.dot_general(
            block, cot[:, i * wide:(i + 1) * wide], NT, preferred_element_type=F32
        )
    sketch = sketch[:rank] + sketch[rank:]
    tok = lax.broadcasted_iota(jnp.int32, (rank, seq), 1)
    mixers = [
        halves(jnp.where(tok < len_ref[e], sketch[:, e * seq:(e + 1) * seq], 0.0))
        for e in range(ex)
    ]

    loads[1].wait()
    for k in order + [0]:
        cols = pl.ds(pl.multiple_of(lax.rem(o + k, outer) * wide, wide), wide)
        for e in range(ex):
            mixed = jnp.dot(
                mixers[e], x[e * seq:(e + 1) * seq, cols], preferred_element_type=F32
            )
            mixed = (mixed[:rank] + mixed[rank:]).astype(BF)
            if k:
                ysend[k, e * rank:(e + 1) * rank] = mixed
            else:
                yrecv[k, e * rank:(e + 1) * rank] = mixed
        if k:
            send(ysend.at[k], yrecv.at[k], y_s.at[k], y_r.at[k], along(k))

    loads[2].wait()
    across = (1 - b) * 2 + c
    for i in range(pieces):
        arrived(piece(across, i), pin_r.at[0, i])
        send(piece(across, i), piece(across, i), pin_s.at[2, i], pin_r.at[2, i], mate_c)
    arrived(pin.at[b * 2 + 1 - c], pin_r.at[1, 0])
    for i in range(pieces):
        arrived(piece((1 - b) * 2 + 1 - c, i), pin_r.at[2, i])
    for k in range(1, outer):
        arrived(yrecv.at[k], y_r.at[k])

    mixed = yrecv[...].reshape(outer * ex * rank, wide)
    split = pin.shape[2] // 2
    own = []
    for h in range(2):
        cols = slice(h * split, (h + 1) * split)
        parts = jnp.zeros((outer * ex * rank, split), F32)
        for j in range(4):
            parts += jnp.dot(
                mixed[:, j * depth:(j + 1) * depth], pin[j, :, cols],
                preferred_element_type=F32,
            )
        for k in order:
            psend[k, :, cols] = parts[k * ex * rank:(k + 1) * ex * rank].astype(BF)
            send(
                psend.at[k, :, cols], precv.at[k, :, cols],
                p_s.at[h, k], p_r.at[h, k], along(outer - k),
            )
        own.append(parts[:ex * rank])
    total = jnp.concatenate(own, axis=1)
    for k in range(1, outer):
        for h in range(2):
            arrived(precv.at[k, :, h * split:(h + 1) * split], p_r.at[h, k])
        total += precv[k].astype(F32)
    total = total * (1.0 / math.sqrt(seq))
    feat_ref[...] = total
    all_ref[me] = total.astype(BF)
    gather(all_ref, fz_s, fz_r, fb_s, fb_r, fc_s, fc_r)
    for copy in sent:
        copy.wait_send()


def gram_kernel(ex, all_ref, feat32_ref, gram_hbm, feat_ref, rows, few, own, tiles, sems):
    me = lax.axis_index("fsdp")
    _, own_rows, kd = tiles.shape
    chunks, height, lanes = rows.shape
    rank = height // (all_ref.shape[0] * ex)
    total = height // rank

    def row_of(ref, r, count):
        return jnp.concatenate(
            [ref[i, pl.ds(r, count, stride=rank), :] for i in range(chunks)], axis=1
        )

    for i in range(chunks):
        cols = slice(i * lanes, (i + 1) * lanes)
        rows[i] = all_ref[:, :, cols].reshape(height, lanes).astype(F32)
        few[i] = feat32_ref[:, cols]
    own[...] = row_of(rows, me * own_rows // kd, total).T
    left = own[pl.ds(pl.multiple_of(lax.rem(me * own_rows, kd), own_rows), own_rows), :]
    left = left.astype(BF)
    writes = []
    for r in range(rank):
        tiles[r] = jnp.dot(
            left, row_of(rows, r, total).astype(BF), preferred_element_type=F32
        ) * (1.0 / total)
        write = pltpu.make_async_copy(
            tiles.at[r], gram_hbm.at[:, r * kd:(r + 1) * kd], sems.at[r]
        )
        write.start()
        writes.append(write)
    for r in range(rank):
        feat_ref[:, r * kd:(r + 1) * kd] = row_of(few, r, ex)
    for write in writes:
        write.wait()


def on_device(inputs, cotangent, up, narrow, projection, lengths):
    devices = lax.axis_size("fsdp")
    outer = devices // 4
    ex = lengths.shape[0]
    tokens, width = inputs.shape
    rank = narrow.shape[1]
    depth, kd = projection.shape
    rows = ex * rank
    vmem = pl.BlockSpec(memory_space=pltpu.VMEM)
    hbm = pl.BlockSpec(memory_space=pltpu.HBM)
    sems = [6]
    sems += [outer, outer, outer, outer, 2 * outer, 2 * outer] * 2
    sems += [(3, 4), (3, 4), outer, outer, (2, outer), (2, outer)]
    feat32, everyone = pl.pallas_call(
        functools.partial(features_kernel, outer),
        out_shape=(
            jax.ShapeDtypeStruct((rows, kd), F32),
            jax.ShapeDtypeStruct((devices, rows, kd), BF),
        ),
        in_specs=[hbm] * 6,
        out_specs=(vmem, vmem),
        scratch_shapes=[
            pltpu.SMEM((ex,), jnp.int32),
            pltpu.VMEM((depth, up.shape[1]), BF),
            pltpu.VMEM((rank, up.shape[1]), BF),
            pltpu.VMEM((tokens, width), BF),
            pltpu.VMEM((tokens, width), BF),
            pltpu.VMEM((devices, 2 * rank, depth), BF),
            pltpu.VMEM((4, depth, kd), BF),
            pltpu.VMEM((outer, rows, 4 * depth), BF),
            pltpu.VMEM((outer, rows, 4 * depth), BF),
            pltpu.VMEM((outer, rows, kd), BF),
            pltpu.VMEM((outer, rows, kd), BF),
        ] + [pltpu.SemaphoreType.DMA(n if isinstance(n, tuple) else (n,)) for n in sems],
        compiler_params=pltpu.CompilerParams(
            collective_id=0, has_side_effects=True, vmem_limit_bytes=63 * 1024 * 1024
        ),
        name="features",
    )(lengths, up, narrow.T, projection, cotangent, inputs)
    own_rows = rank * kd // devices
    total = ex * devices
    gram, features = pl.pallas_call(
        functools.partial(gram_kernel, ex),
        out_shape=(
            jax.ShapeDtypeStruct((own_rows, rank * kd), F32),
            jax.ShapeDtypeStruct((ex, rank * kd), F32),
        ),
        in_specs=[vmem, vmem],
        out_specs=(hbm, vmem),
        scratch_shapes=[
            pltpu.VMEM((kd // 128, total * rank, 128), F32),
            pltpu.VMEM((kd // 128, rows, 128), F32),
            pltpu.VMEM((kd, total), F32),
            pltpu.VMEM((rank, own_rows, kd), F32),
            pltpu.SemaphoreType.DMA((rank,)),
        ],
        compiler_params=pltpu.CompilerParams(vmem_limit_bytes=63 * 1024 * 1024),
        name="gram",
    )(everyone, feat32)
    return features, gram


def solution(mesh):
    rows = P(("parts", "fsdp"), None)
    in_specs = (rows, rows, P("fsdp", None), P(), P("fsdp", None), P(("parts", "fsdp")))
    return jax.shard_map(
        on_device, mesh=mesh, in_specs=in_specs, out_specs=(rows, rows), check_vma=False
    )
```

```python
import functools
import math

import jax
import jax.numpy as jnp
from jax import lax
from jax.experimental import pallas as pl
from jax.experimental.pallas import tpu as pltpu
from jax.sharding import PartitionSpec as P

BF = jnp.bfloat16
F32 = jnp.float32
NT = (((1,), (1,)), ((), ()))


def halves(value):
    high = value.astype(BF)
    low = (value - high.astype(F32)).astype(BF)
    return jnp.concatenate([high, low], axis=0)


def features_kernel(
    outer,
    len_hbm, up_hbm, narrow_hbm, proj_ref, cot_hbm, x_hbm,
    feat_ref, all_ref,
    len_ref, up_ref, narrow_ref, cot, x, folded, pin, ysend, yrecv, psend, precv,
    local_sem, bz_s, bz_r, bb_s, bb_r, bc_s, bc_r,
    fz_s, fz_r, fb_s, fb_r, fc_s, fc_r, pin_s, pin_r, y_s, y_r, p_s, p_r,
):
    me = lax.axis_index("fsdp")
    o, within = me // 4, me % 4
    b, c = within // 2, within % 2
    plane = within
    mate_b = o * 4 + (1 - b) * 2 + c
    mate_c = o * 4 + b * 2 + (1 - c)
    rank = narrow_ref.shape[0]
    ex = len_ref.shape[0]
    seq = x.shape[0] // ex
    wide = ysend.shape[2]

    def along(step):
        return lax.rem(o + step, outer) * 4 + plane

    early = [
        pltpu.make_async_copy(up_hbm, up_ref, local_sem.at[3]),
        pltpu.make_async_copy(narrow_hbm, narrow_ref, local_sem.at[4]),
        pltpu.make_async_copy(len_hbm, len_ref, local_sem.at[5]),
    ]
    loads = [
        pltpu.make_async_copy(cot_hbm, cot, local_sem.at[0]),
        pltpu.make_async_copy(x_hbm, x, local_sem.at[1]),
        pltpu.make_async_copy(proj_ref, pin.at[plane], local_sem.at[2]),
    ]
    for load in early + loads:
        load.start()

    barrier = pltpu.get_barrier_semaphore()
    for other in [along(k) for k in range(1, outer)] + [mate_b, mate_c]:
        pl.semaphore_signal(
            barrier, inc=1, device_id={"fsdp": other}, device_id_type=pl.DeviceIdType.MESH
        )

    for load in early:
        load.wait()
    part = lax.dot_general(narrow_ref[...], up_ref[...], NT, preferred_element_type=F32)
    folded[me] = part.astype(BF)
    pl.semaphore_wait(barrier, outer + 1)

    sent = []
    order = sorted(range(1, outer), key=lambda k: abs(k - outer // 2))

    def send(src, dst, s_sem, r_sem, other):
        copy = pltpu.make_async_remote_copy(
            src_ref=src, dst_ref=dst, send_sem=s_sem, recv_sem=r_sem,
            device_id={"fsdp": other}, device_id_type=pl.DeviceIdType.MESH,
        )
        copy.start()
        sent.append(copy)

    def arrived(dst, sem):
        pltpu.make_async_copy(dst, dst, sem).wait()

    def gather(buf, z_s, z_r, b_s, b_r, c_s, c_r):
        for k in range(1, outer):
            send(buf.at[me], buf.at[me], z_s.at[k], z_r.at[k], along(k))
        send(buf.at[me], buf.at[me], b_s.at[0], b_r.at[0], mate_b)
        send(buf.at[me], buf.at[me], c_s.at[0], c_r.at[0], mate_c)
        for k in reversed(order):
            slot = along(outer - k)
            arrived(buf.at[slot], z_r.at[k])
            send(buf.at[slot], buf.at[slot], b_s.at[k], b_r.at[k], mate_b)
            send(buf.at[slot], buf.at[slot], c_s.at[k], c_r.at[k], mate_c)
        for k in range(outer):
            slot = lax.rem(o + outer - k, outer) * 4 + (1 - b) * 2 + c
            arrived(buf.at[slot], b_r.at[k])
            send(buf.at[slot], buf.at[slot], c_s.at[outer + k], c_r.at[outer + k], mate_c)
        for half in range(2):
            for k in range(outer):
                arrived(buf.at[me], c_r.at[half * outer + k])

    depth = wide // 4
    pieces = 4
    high = depth // pieces

    def piece(slot, i):
        return pin.at[slot, pl.ds(i * high, high)]

    def pin_start(i):
        source = proj_ref.at[pl.ds(i * high, high)]
        send(source, piece(plane, i), pin_s.at[0, i], pin_r.at[0, i], mate_b)

    pin_start(0)
    gather(folded, bz_s, bz_r, bb_s, bb_r, bc_s, bc_r)
    for i in range(1, pieces):
        pin_start(i)
    send(proj_ref, pin.at[plane], pin_s.at[1, 0], pin_r.at[1, 0], mate_c)

    loads[0].wait()
    sketch = jnp.zeros((rank, x.shape[0]), F32)
    for i in range(outer):
        block = jnp.concatenate([folded[i * 4 + j] for j in range(4)], axis=1)
        sketch += lax.dot_general(
            block, cot[:, i * wide:(i + 1) * wide], NT, preferred_element_type=F32
        )
    tok = lax.broadcasted_iota(jnp.int32, (rank, seq), 1)
    mixers = [
        halves(jnp.where(tok < len_ref[e], sketch[:, e * seq:(e + 1) * seq], 0.0))
        for e in range(ex)
    ]

    loads[1].wait()
    for k in order + [0]:
        cols = pl.ds(pl.multiple_of(lax.rem(o + k, outer) * wide, wide), wide)
        for e in range(ex):
            mixed = jnp.dot(
                mixers[e], x[e * seq:(e + 1) * seq, cols], preferred_element_type=F32
            )
            mixed = (mixed[:rank] + mixed[rank:]).astype(BF)
            if k:
                ysend[k, e * rank:(e + 1) * rank] = mixed
            else:
                yrecv[k, e * rank:(e + 1) * rank] = mixed
        if k:
            send(ysend.at[k], yrecv.at[k], y_s.at[k], y_r.at[k], along(k))

    loads[2].wait()
    across = (1 - b) * 2 + c
    for i in range(pieces):
        arrived(piece(across, i), pin_r.at[0, i])
        send(piece(across, i), piece(across, i), pin_s.at[2, i], pin_r.at[2, i], mate_c)
    arrived(pin.at[b * 2 + 1 - c], pin_r.at[1, 0])
    for i in range(pieces):
        arrived(piece((1 - b) * 2 + 1 - c, i), pin_r.at[2, i])
    for k in range(1, outer):
        arrived(yrecv.at[k], y_r.at[k])

    mixed = yrecv[...].reshape(outer * ex * rank, wide)
    split = pin.shape[2] // 2
    own = []
    for h in range(2):
        cols = slice(h * split, (h + 1) * split)
        parts = jnp.zeros((outer * ex * rank, split), F32)
        for j in range(4):
            parts += jnp.dot(
                mixed[:, j * depth:(j + 1) * depth], pin[j, :, cols],
                preferred_element_type=F32,
            )
        for k in order:
            psend[k, :, cols] = parts[k * ex * rank:(k + 1) * ex * rank].astype(BF)
            send(
                psend.at[k, :, cols], precv.at[k, :, cols],
                p_s.at[h, k], p_r.at[h, k], along(outer - k),
            )
        own.append(parts[:ex * rank])
    total = jnp.concatenate(own, axis=1)
    for k in range(1, outer):
        for h in range(2):
            arrived(precv.at[k, :, h * split:(h + 1) * split], p_r.at[h, k])
        total += precv[k].astype(F32)
    total = total * (1.0 / math.sqrt(seq))
    feat_ref[...] = total
    all_ref[me] = total.astype(BF)
    gather(all_ref, fz_s, fz_r, fb_s, fb_r, fc_s, fc_r)
    for copy in sent:
        copy.wait_send()


def gram_kernel(ex, all_ref, feat32_ref, gram_hbm, feat_ref, rows, few, own, tiles, sems):
    me = lax.axis_index("fsdp")
    _, own_rows, kd = tiles.shape
    chunks, height, lanes = rows.shape
    rank = height // (all_ref.shape[0] * ex)
    total = height // rank

    def row_of(ref, r, count):
        return jnp.concatenate(
            [ref[i, pl.ds(r, count, stride=rank), :] for i in range(chunks)], axis=1
        )

    for i in range(chunks):
        cols = slice(i * lanes, (i + 1) * lanes)
        rows[i] = all_ref[:, :, cols].reshape(height, lanes).astype(F32)
        few[i] = feat32_ref[:, cols]
    own[...] = row_of(rows, me * own_rows // kd, total).T
    left = own[pl.ds(pl.multiple_of(lax.rem(me * own_rows, kd), own_rows), own_rows), :]
    left = left.astype(BF)
    writes = []
    for r in range(rank):
        tiles[r] = jnp.dot(
            left, row_of(rows, r, total).astype(BF), preferred_element_type=F32
        ) * (1.0 / total)
        write = pltpu.make_async_copy(
            tiles.at[r], gram_hbm.at[:, r * kd:(r + 1) * kd], sems.at[r]
        )
        write.start()
        writes.append(write)
    for r in range(rank):
        feat_ref[:, r * kd:(r + 1) * kd] = row_of(few, r, ex)
    for write in writes:
        write.wait()


def on_device(inputs, cotangent, up, narrow, projection, lengths):
    devices = lax.axis_size("fsdp")
    outer = devices // 4
    ex = lengths.shape[0]
    tokens, width = inputs.shape
    rank = narrow.shape[1]
    depth, kd = projection.shape
    rows = ex * rank
    vmem = pl.BlockSpec(memory_space=pltpu.VMEM)
    hbm = pl.BlockSpec(memory_space=pltpu.HBM)
    sems = [6]
    sems += [outer, outer, outer, outer, 2 * outer, 2 * outer] * 2
    sems += [(3, 4), (3, 4), outer, outer, (2, outer), (2, outer)]
    feat32, everyone = pl.pallas_call(
        functools.partial(features_kernel, outer),
        out_shape=(
            jax.ShapeDtypeStruct((rows, kd), F32),
            jax.ShapeDtypeStruct((devices, rows, kd), BF),
        ),
        in_specs=[hbm] * 6,
        out_specs=(vmem, vmem),
        scratch_shapes=[
            pltpu.SMEM((ex,), jnp.int32),
            pltpu.VMEM((depth, up.shape[1]), BF),
            pltpu.VMEM((rank, up.shape[1]), BF),
            pltpu.VMEM((tokens, width), BF),
            pltpu.VMEM((tokens, width), BF),
            pltpu.VMEM((devices, rank, depth), BF),
            pltpu.VMEM((4, depth, kd), BF),
            pltpu.VMEM((outer, rows, 4 * depth), BF),
            pltpu.VMEM((outer, rows, 4 * depth), BF),
            pltpu.VMEM((outer, rows, kd), BF),
            pltpu.VMEM((outer, rows, kd), BF),
        ] + [pltpu.SemaphoreType.DMA(n if isinstance(n, tuple) else (n,)) for n in sems],
        compiler_params=pltpu.CompilerParams(
            collective_id=0, has_side_effects=True, vmem_limit_bytes=63 * 1024 * 1024
        ),
        name="features",
    )(lengths, up, narrow.T, projection, cotangent, inputs)
    own_rows = rank * kd // devices
    total = ex * devices
    gram, features = pl.pallas_call(
        functools.partial(gram_kernel, ex),
        out_shape=(
            jax.ShapeDtypeStruct((own_rows, rank * kd), F32),
            jax.ShapeDtypeStruct((ex, rank * kd), F32),
        ),
        in_specs=[vmem, vmem],
        out_specs=(hbm, vmem),
        scratch_shapes=[
            pltpu.VMEM((kd // 128, total * rank, 128), F32),
            pltpu.VMEM((kd // 128, rows, 128), F32),
            pltpu.VMEM((kd, total), F32),
            pltpu.VMEM((rank, own_rows, kd), F32),
            pltpu.SemaphoreType.DMA((rank,)),
        ],
        compiler_params=pltpu.CompilerParams(vmem_limit_bytes=63 * 1024 * 1024),
        name="gram",
    )(everyone, feat32)
    return features, gram


def solution(mesh):
    rows = P(("parts", "fsdp"), None)
    in_specs = (rows, rows, P("fsdp", None), P(), P("fsdp", None), P(("parts", "fsdp")))
    return jax.shard_map(
        on_device, mesh=mesh, in_specs=in_specs, out_specs=(rows, rows), check_vma=False
    )
```
